512 devices in a mesh: seq: 128 (over z, x, core), batch: 4 (over y).
Axes of the slice: x: 4, y: 4, z: 16, core: 2. Of those that a mesh axis runs over, the one named last changes fastest.
Arguments:
- tokens: bfloat16 [4, 128, 128, 1152], P('batch', 'seq'), may hold values from -6 to 6
- spatial_query: bfloat16 [4, 128, 128, 1152], P('batch', 'seq'), may hold values from -24 to 24
- spatial_key: bfloat16 [4, 128, 128, 1152], P('batch', 'seq'), may hold values from -24 to 24
- spatial_value: bfloat16 [4, 128, 128, 1152], P('batch', 'seq'), may hold values from -6 to 6
- frame_counts: int32 [4, 16], P('batch'), may hold values from 1 to 64, 128 in all within a row
- w_spatial_out: bfloat16 [1152, 1152], P('seq', 'batch'), may hold values from -0.1875 to 0.1875
- w_temporal_qkv: bfloat16 [1152, 3456], P('seq', 'batch'), may hold values from -3 to 3
- w_temporal_out: bfloat16 [1152, 1152], P('seq', 'batch'), may hold values from -0.1875 to 0.1875
Outputs:
- block_out: bfloat16 [4, 128, 128, 1152], P('batch', 'seq')
The draws below stay inside these ranges and needn't reach their ends.
Inputs may be any that keep to these rules, and one draw needn't show every extreme that they name: `frame_counts`: the counts of a group sum to 128; one clip has exactly 64 frames.
All inputs are finite; a program needn't handle non-finite values.
Results may differ from the reference program's by a relative error of at most 0.015.
Values may be sent and summed in bfloat16 or wider, within the bound.
A program may use at most 128 MiB of HBM per device.

```python
import math
import jax
import jax.numpy as jnp
import numpy as np
from jax import lax

D = 1152
HEADS = 16
HEAD_SIZE = 72
P_SIZE = 128
GROUPS = 4
FRAMES = 128
CLIPS = 16
MOST = 64


def draw_spatial_query(key, part):
    key = jax.random.fold_in(key, 11)
    drawn = jnp.clip(jax.random.normal(key, (GROUPS, FRAMES, P_SIZE, D), jnp.float32), -4.0, 4.0)
    return drawn.astype(jnp.bfloat16)


def draw_spatial_key(key, part):
    key = jax.random.fold_in(key, 12)
    drawn = jnp.clip(jax.random.normal(key, (GROUPS, FRAMES, P_SIZE, D), jnp.float32), -4.0, 4.0)
    return drawn.astype(jnp.bfloat16)


def draw_w_temporal_qkv(key, part):
    key = jax.random.fold_in(key, 21)
    drawn = jnp.clip(jax.random.normal(key, (D, 3 * D), jnp.float32), -4.0, 4.0) * (1.0 / D ** 0.5)
    return drawn.astype(jnp.bfloat16)


def shard_levels(rng, shape, shards, low, top_value):
    loudness = 1.0
    for dim, blocks in shards:
        draws = jax.random.uniform(jax.random.fold_in(jax.random.fold_in(rng, 6), dim), (blocks,), jnp.float32, low / len(shards), top_value / len(shards))
        loudness = loudness * jnp.repeat(jnp.exp(draws), shape[dim] // blocks).reshape((-1,) + (1,) * (len(shape) - 1 - dim))
    return loudness


def length_profile(number_of, total, reach, slope):
    weights = [(1 << 20) // math.isqrt(rank ** slope) + 1 for rank in range(2, number_of + 1)]
    spare, holding = total - reach - (number_of - 1), [1] * (number_of - 1)
    while spare > 0:
        free = [i for i in range(number_of - 1) if holding[i] < reach]
        whole, left = sum([weights[i] for i in free]), spare
        for i in free:
            extra = min(reach - holding[i], max(1, left * weights[i] // whole), spare)
            holding[i] = holding[i] + extra
            spare = spare - extra
    return np.array([reach] + holding)


def uneven_parts(stream_key, count, total, reach, skew):
    if count == 2:
        one = jax.random.randint(stream_key, (), max(1, total - reach), min(reach, total - 1) + 1)
        return jnp.stack([one, total - one])
    lengths = jnp.asarray(length_profile(count, total, reach, skew), jnp.int32)
    pairs = (count - 1) // 2
    donor, receiver = lengths[1:1 + 2 * pairs:2], lengths[2:2 + 2 * pairs:2]
    slack = jnp.minimum(donor - 1, reach - receiver)
    moved = jax.random.randint(jax.random.fold_in(stream_key, 1), (pairs,), 0, 1 << 20) % (slack + 1)
    lengths = lengths.at[1:1 + 2 * pairs:2].set(donor - moved).at[2:2 + 2 * pairs:2].set(receiver + moved)
    return lengths[jax.random.permutation(jax.random.fold_in(stream_key, 2), count)]


def bell_draw(rng, shape, scale, limit, shards=(), kind=jnp.bfloat16):
    drawn = jax.random.normal(rng, shape, jnp.float32) * scale
    if len(shards) > 0:
        drawn = shard_levels(rng, shape, shards, -0.22, 0.18) * drawn
    return jnp.clip(drawn, min=-limit, max=limit).astype(kind)


def setup_inputs(seed: int = 0) -> dict:
    key_of = jax.random.split(jax.random.key(seed), 9)
    tokens = bell_draw(key_of[0], (GROUPS, FRAMES, P_SIZE, D), 1.0, 6.0, ((0, 4), (1, 128)))
    spatial_query = draw_spatial_query(jax.random.fold_in(key_of[8], 71), 0)
    spatial_key = draw_spatial_key(jax.random.fold_in(key_of[8], 71), 0)
    spatial_value = bell_draw(key_of[3], (GROUPS, FRAMES, P_SIZE, D), 1.0, 6.0, ((0, 4), (1, 128)))
    frame_counts = jax.vmap(lambda own: uneven_parts(own, CLIPS, FRAMES, MOST, 2))(jax.random.split(key_of[4], GROUPS)).reshape((GROUPS, CLIPS)).astype(jnp.int32)
    w_spatial_out = bell_draw(key_of[5], (D, D), D ** -0.5, 0.1875, ((0, 128), (1, 4)))
    w_temporal_qkv = draw_w_temporal_qkv(jax.random.fold_in(key_of[8], 71), 0)
    w_temporal_out = bell_draw(key_of[7], (D, D), D ** -0.5, 0.1875, ((0, 128), (1, 4)))
    return dict(tokens=tokens, spatial_query=spatial_query, spatial_key=spatial_key, spatial_value=spatial_value, frame_counts=frame_counts, w_spatial_out=w_spatial_out, w_temporal_qkv=w_temporal_qkv, w_temporal_out=w_temporal_out)


EPS = 1e-06

def clip_ids(counts, frames):
    ends = jnp.cumsum(counts).astype(jnp.int32)
    index = jnp.arange(frames, dtype=jnp.int32)
    return lax.optimization_barrier(jnp.sum((index[:, None] >= ends[None, :]).astype(jnp.int32), axis=1)).astype(jnp.int32)

def spatial_frame(items):
    query, keyed, value = items
    shape = (P_SIZE, HEADS, HEAD_SIZE)
    query = query.reshape(shape).astype(jnp.float32)
    keyed = keyed.reshape(shape).astype(jnp.float32)
    value = value.reshape(shape).astype(jnp.float32)
    scores = jnp.einsum('phd,qhd->hpq', query, keyed) / jnp.sqrt(jnp.float32(HEAD_SIZE))
    weights = jax.nn.softmax(scores, axis=-1).astype(jnp.bfloat16)
    context = jnp.einsum('hpq,qhd->phd', weights.astype(jnp.float32), value)
    return context.reshape(P_SIZE, D).astype(jnp.bfloat16)

def one_group(items, w_spatial_out, w_temporal_qkv, w_temporal_out):
    tokens, query, keyed, value, counts = items
    context = lax.map(spatial_frame, (query, keyed, value))
    rows = FRAMES * P_SIZE
    flat = tokens.reshape(rows, D).astype(jnp.float32)
    hidden = (flat + jnp.dot(context.reshape(rows, D), w_spatial_out, preferred_element_type=jnp.float32)).astype(jnp.bfloat16)
    wide = hidden.astype(jnp.float32)
    mean = lax.optimization_barrier(jnp.mean(wide, axis=1, keepdims=True))
    var = lax.optimization_barrier(jnp.mean((wide - mean) ** 2, axis=1, keepdims=True))
    normed = ((wide - mean) * lax.rsqrt(var + EPS)).astype(jnp.bfloat16)
    qkv = jnp.dot(normed, w_temporal_qkv, preferred_element_type=jnp.float32)
    shape = (FRAMES, P_SIZE, HEADS, HEAD_SIZE)
    t_query = qkv[:, :D].astype(jnp.bfloat16).reshape(shape).transpose(1, 0, 2, 3)
    t_key = qkv[:, D:2 * D].astype(jnp.bfloat16).reshape(shape).transpose(1, 0, 2, 3)
    t_value = qkv[:, 2 * D:].astype(jnp.bfloat16).reshape(shape).transpose(1, 0, 2, 3)
    clip = clip_ids(counts, FRAMES)
    same = clip[:, None] == clip[None, :]

    def position(parts):
        tq, tk, tv = parts
        scores = jnp.einsum('fhd,ghd->hfg', tq.astype(jnp.float32), tk.astype(jnp.float32)) / jnp.sqrt(jnp.float32(HEAD_SIZE))
        scores = jnp.where(same[None], scores, jnp.float32(-1e+30))
        weights = jax.nn.softmax(scores, axis=-1).astype(jnp.bfloat16)
        return jnp.einsum('hfg,ghd->fhd', weights.astype(jnp.float32), tv.astype(jnp.float32)).astype(jnp.bfloat16)
    temporal = lax.map(position, (t_query, t_key, t_value))
    temporal = temporal.transpose(1, 0, 2, 3).reshape(rows, D)
    out = hidden.astype(jnp.float32) + jnp.dot(temporal, w_temporal_out, preferred_element_type=jnp.float32)
    return out.astype(jnp.bfloat16).reshape(FRAMES, P_SIZE, D)

def reference(tokens, spatial_query, spatial_key, spatial_value, frame_counts, w_spatial_out, w_temporal_qkv, w_temporal_out):
    return lax.map(lambda items: one_group(items, w_spatial_out, w_temporal_qkv, w_temporal_out), (tokens, spatial_query, spatial_key, spatial_value, frame_counts))
```

```python
import jax
import jax.numpy as jnp
from jax import lax
from jax.experimental import pallas as pl
from jax.experimental.pallas import tpu as pltpu
from jax.sharding import PartitionSpec as P

HEADS = 16
EPS = 1e-06
MESH = pl.DeviceIdType.MESH
BF16 = jnp.bfloat16
F32 = jnp.float32

ROWS = 128
WIDTH = 1152
SIZE = WIDTH // HEADS
LANES = 128
RAW = 1792
STEPS = 3
PAIR = 144


def dot(left, right):
    return jnp.dot(left, right, preferred_element_type=F32)


def iota(shape, dim):
    return lax.broadcasted_iota(jnp.int32, shape, dim)


def layer_norm(wide):
    mean = jnp.mean(wide, axis=1, keepdims=True)
    var = jnp.mean((wide - mean) ** 2, axis=1, keepdims=True)
    return ((wide - mean) * lax.rsqrt(var + EPS)).astype(BF16)


def attention(q_ref, k_ref, v_ref, same):
    scale = SIZE**-0.5
    parts = [[] for _ in range(WIDTH // LANES)]
    for head in range(HEADS):
        low = SIZE * head
        start = low // LANES * LANES
        span = LANES if low + SIZE <= start + LANES else 2 * LANES
        window = slice(start, start + span)
        lane = iota((1, span), 1) + start
        own = jnp.where((lane >= low) & (lane < low + SIZE), 1.0, 0.0).astype(BF16)
        scores = lax.dot_general(
            q_ref[:, window] * own, k_ref[:, window], (((1,), (1,)), ((), ())), preferred_element_type=F32
        )
        scores = scores * scale
        if same is not None:
            scores = jnp.where(same, scores, -1e30)
        top = jnp.max(scores, axis=1, keepdims=True)
        raised = jnp.exp(scores - top)
        weights = (raised * (1.0 / jnp.sum(raised, axis=1, keepdims=True))).astype(BF16)
        context = dot(weights, v_ref[:, window])
        for tile in range(span // LANES):
            parts[start // LANES + tile].append(
                (low + SIZE, context[:, tile * LANES : (tile + 1) * LANES])
            )
    lane = iota((ROWS, LANES), 1)
    tiles = []
    for index, found in enumerate(parts):
        total = found[-1][1]
        for end, value in reversed(found[:-1]):
            total = jnp.where(lane + index * LANES < end, value, total)
        tiles.append(total)
    return tiles


def kernel(
    counts, tok, sq, sk, sv, wraw, out,
    raw, piece, gat, wts, tokp, ctx, ctxp, zt, zc, xst, xsc, xrt, xrc,
    hid_f, hid_p, normed, qkv, tctx, rback, plane, zback,
    y_s, y_r, g_s, g_r, p_s, p_r, w_s, w_r, z_s, z_r, x_s, x_r,
):
    me = lax.axis_index("seq")
    y = lax.axis_index("batch")
    z = lax.div(me, 8)
    xc = lax.rem(me, 8)
    x = lax.div(xc, 2)
    c = lax.rem(me, 2)
    zp = lax.div(z, 2)
    zpar = lax.rem(z, 2)
    zmate = z + 1 - 2 * zpar
    cstar = lax.div(z, 8)
    active = c == cstar

    def at(z2, xc2, y2):
        return {"seq": z2 * 8 + xc2, "batch": y2}

    def ring(value, step, size):
        return lax.rem(value + (step + size), size)

    def remote(src, dst, send, recv, device):
        return pltpu.make_async_remote_copy(
            src_ref=src, dst_ref=dst, send_sem=send, recv_sem=recv, device_id=device, device_id_type=MESH
        )

    sends = []

    def send(src, dst, ss, rs, device):
        copy = remote(src, dst, ss, rs, device)
        copy.start()
        sends.append(copy)

    def arrived(dst, ss, rs):
        remote(dst, dst, ss, rs, at(z, xc, y)).wait_recv()

    barrier = pltpu.get_barrier_semaphore()
    peers = [at(z, xc, ring(y, d, 4)) for d in (1, 2, 3)]
    peers += [at(z, ring(xc, d, 8), y) for d in range(1, 8)]
    peers += [at(zmate, ring(xc, d, 8), y) for d in range(1, 8)]
    peers += [at(ring(z, d, 16), xc, y) for d in range(1, 16)]
    for peer in peers:
        pl.semaphore_signal(barrier, inc=1, device_id=peer, device_id_type=MESH)

    raw[y] = wraw[...]
    wide = tok[...].astype(F32)
    for i in range(16):
        tokp[i] = wide[8 * i : 8 * i + 8].astype(BF16)
    for i, tile in enumerate(attention(sq, sk, sv, None)):
        ctx[:, i * LANES : (i + 1) * LANES] = tile.astype(BF16)
        for r in range(16):
            ctxp[r, :, i * LANES : (i + 1) * LANES] = tile[8 * r : 8 * r + 8].astype(BF16)

    pl.semaphore_wait(barrier, len(peers))

    for d in (1, 2, 3):
        send(raw.at[y], raw.at[y], y_s.at[d], y_r.at[y], at(z, xc, ring(y, d, 4)))

    def z_exchange(n, src, dst):
        for d in range(1, 16):
            to = ring(z, d, 16)
            send(src.at[to], dst.at[z], z_s.at[n, d], z_r.at[n, z], at(to, xc, y))
        dst[z] = src[z]

    def z_wait(n, dst):
        for d in range(1, 16):
            source = ring(z, d, 16)
            arrived(dst.at[source], z_s.at[n, d], z_r.at[n, source])

    def x_exchange(n, src, dst):
        for d in range(1, 8):
            to = ring(xc, d, 8)
            send(src.at[to], dst.at[xc], x_s.at[n, d], x_r.at[n, xc], at(z, to, y))
        dst[xc] = src[xc]

    def x_wait(n, dst):
        for d in range(1, 8):
            source = ring(xc, d, 8)
            arrived(dst.at[source], x_s.at[n, d], x_r.at[n, source])

    def rows_of(ref):
        return jnp.concatenate([ref[i].astype(F32) for i in range(16)], axis=0).astype(BF16)

    def swap_rows(left, inner):
        outer = ROWS // inner
        i, k = iota((ROWS, ROWS), 0), iota((ROWS, ROWS), 1)
        pick = k == lax.rem(i, inner) * outer + lax.div(i, inner)
        return dot(jnp.where(pick, 1.0, 0.0).astype(BF16), left)

    z_exchange(0, tokp, zt)

    for d in (1, 2, 3):
        source = ring(y, d, 4)
        arrived(raw.at[source], y_s.at[d], y_r.at[source])

    row, col = iota((3 * LANES, LANES), 0), iota((3 * LANES, LANES), 1)
    for j in range(STEPS):
        for x2 in range(4):
            tile = jnp.minimum(16 * j + 4 * x2 + y, 44)
            second = jnp.where(tile >= 9, 1, 0)
            third = jnp.where(tile >= 36, 1, 0)
            block = 288 + 576 * (second - third)
            lanes = 384 * second + 896 * third
            begin = LANES * (tile - 9 * second - 27 * third)
            y1 = jnp.where(second - third == 1, lax.div(begin, 864), lax.div(begin, 288))
            y2 = jnp.minimum(y1 + 1, 3)
            inside = begin - y1 * block
            skip = lax.rem(inside, LANES)
            first = jnp.minimum(block - inside, LANES)
            near = (row == col + skip) & (col < first)
            far = (row == col - first + 2 * LANES) & (col >= first)
            pick = jnp.where(near | far, 1.0, 0.0).astype(BF16)
            start = pl.multiple_of(lanes + inside - skip, LANES)
            left = raw[y1, :, pl.ds(start, 2 * LANES)]
            right = raw[y2, :, pl.ds(pl.multiple_of(lanes, LANES), LANES)]
            piece[x2, j] = dot(jnp.concatenate([left, right], axis=1), pick).astype(BF16)

    source = 8 * zpar + xc
    for zo in (0, 1):
        for dx in range(4):
            x2 = ring(x, dx, 4)
            where = at(z if zo == 0 else zmate, 2 * x2 + cstar, y)
            sem = g_s.at[4 * zo + dx]
            if zo == 0 and dx == 0:

                @pl.when(active)
                def _():
                    gat[source] = piece[x]

                @pl.when(jnp.logical_not(active))
                def _():
                    remote(piece.at[x2], gat.at[source], sem, g_r.at[source], where).start()
            else:
                send(piece.at[x2], gat.at[source], sem, g_r.at[source], where)

    @pl.when(active)
    def _():
        for d in range(1, 16):
            other = ring(source, d, 16)
            arrived(gat.at[other], g_s.at[0], g_r.at[other])
        i, k = iota((PAIR, 256), 0), iota((PAIR, 256), 1)
        pick = jnp.where(k == 16 * lax.div(i, 9) + lax.rem(i, 9), 1.0, 0.0).astype(BF16)
        for j in range(STEPS):
            wts[j, x, y, zp] = dot(pick, gat[:, j].reshape(256, LANES)).astype(BF16)
            for d in range(1, 8):
                to = ring(z, d * (2 * zpar - 1), 16)
                spot = wts.at[j, x, y, zp]
                remote(spot, spot, p_s.at[j, d], p_r.at[j, zp], at(to, xc, y)).start()

    z_exchange(1, ctxp, zc)

    up, down = (lambda v: ring(v, 1, 4)), (lambda v: ring(v, -1, 4))
    far = lambda v: ring(v, 2, 4)

    def chain(j, order):
        base = 4 * c + 2 * order
        both, low, high = pl.ds(base, 2), pl.ds(base, 1), pl.ds(base + 1, 1)
        u, v = (x, y) if order == 0 else (y, x)

        def ref(uu, vv, part):
            if order == 0:
                return wts.at[j, uu, vv, part]
            return wts.at[j, vv, uu, part]

        def line(vv, part):
            if order == 0:
                return wts.at[j, :, vv, part]
            return wts.at[j, vv, :, part]

        def device(uu, vv):
            return at(z, 2 * uu + c, vv) if order == 0 else at(z, 2 * vv + c, uu)

        def go(n, spot, uu, vv):
            send(spot, spot, w_s.at[j, order, n], w_r.at[j, order, n], device(uu, vv))

        def got(n, spot):
            arrived(spot, w_s.at[j, order, n], w_r.at[j, order, n])

        def share(n, spot):
            send(spot, spot, w_s.at[j, order, n], w_r.at[j, order, n], at(z, 2 * x + 1 - c, y))

        def shared(n, vv):
            spot = (
                wts.at[j, :, vv, pl.ds(4 * (1 - c) + 2 * order, 2)]
                if order == 0
                else wts.at[j, vv, :, pl.ds(4 * (1 - c) + 2 * order, 2)]
            )
            arrived(spot, w_s.at[j, order, n], w_r.at[j, order, n])

        def s0():
            go(0, ref(u, v, both), up(u), v)
            go(1, ref(u, v, both), down(u), v)
            go(4, ref(u, v, both), u, up(v))
            go(5, ref(u, v, both), u, down(v))

        def s1():
            got(0, ref(down(u), v, both))
            go(2, ref(down(u), v, low), up(u), v)
            go(6, ref(down(u), v, both), u, up(v))
            go(7, ref(down(u), v, both), u, down(v))
            got(1, ref(up(u), v, both))
            go(3, ref(up(u), v, high), down(u), v)
            go(8, ref(up(u), v, both), u, up(v))
            go(9, ref(up(u), v, both), u, down(v))

        def s2():
            got(2, ref(far(u), v, low))
            got(3, ref(far(u), v, high))
            go(10, ref(far(u), v, both), u, up(v))
            go(11, ref(far(u), v, both), u, down(v))
            share(14, line(v, both))

        def s3():
            for k, uu in enumerate((u, down(u), up(u), far(u))):
                got(4 + 2 * k, ref(uu, down(v), both))
            go(12, line(down(v), low), u, up(v))
            share(15, line(down(v), both))
            for k, uu in enumerate((u, down(u), up(u), far(u))):
                got(5 + 2 * k, ref(uu, up(v), both))
            go(13, line(up(v), high), u, down(v))
            share(16, line(up(v), both))

        def s4():
            got(12, line(far(v), low))
            got(13, line(far(v), high))
            share(17, line(far(v), both))

        def s5():
            shared(14, v)
            shared(15, down(v))
            shared(16, up(v))
            shared(17, far(v))

        return s0, s1, s2, s3, s4, s5

    chains = [[chain(j, 0), chain(j, 1)] for j in range(STEPS)]

    def stage(j, s):
        if s == 0:
            for k in range(4):

                @pl.when(4 * c + k != zp)
                def _():
                    arrived(wts.at[j, x, y, 4 * c + k], p_s.at[j, 1], p_r.at[j, 4 * c + k])
        chains[j][0][s]()
        chains[j][1][s]()

    def tiles(left, first, count, emit):
        def body(n, carry):
            right = []
            for i in range(3):
                t = first + 3 * n + i
                k = lax.rem(t, 16)
                right.append(wts[lax.div(t, 16), lax.div(k, 4), lax.rem(k, 4)].reshape(WIDTH, LANES))
            emit(n, dot(left[...], jnp.concatenate(right, axis=1)))
            return carry

        lax.fori_loop(0, count, body, 0)

    def columns(n):
        return pl.ds(pl.multiple_of(n * 384, LANES), 384)

    stage(0, 0)
    stage(0, 1)
    stage(0, 2)
    stage(1, 0)

    z_wait(0, zt)
    moved = swap_rows(rows_of(zt), 16)
    for i in range(8):
        xst[i] = moved[16 * i : 16 * i + 16].astype(BF16)
    x_exchange(0, xst, xrt)

    stage(0, 3)
    stage(1, 1)
    stage(2, 0)

    z_wait(1, zc)
    moved = swap_rows(rows_of(zc), 16)
    for i in range(8):
        xsc[i] = moved[16 * i : 16 * i + 16].astype(BF16)
    x_exchange(1, xsc, xrc)

    stage(0, 4)
    stage(1, 2)
    stage(2, 1)
    stage(0, 5)
    stage(1, 3)
    stage(2, 2)

    def clip_of(dim):
        place = iota((ROWS, ROWS), dim)
        frame = lax.rem(place, 16) * 8 + lax.div(place, 16)
        end = jnp.int32(0)
        clip = jnp.zeros((ROWS, ROWS), jnp.int32)
        for n in range(16):
            end = end + counts[0, n]
            clip = clip + jnp.where(frame >= end, 1, 0)
        return clip

    same = clip_of(0) == clip_of(1)

    x_wait(0, xrt)
    x_wait(1, xrc)

    def hidden_here(n, product):
        hid_f[:, columns(n)] = (tok[:, columns(n)].astype(F32) + product).astype(BF16)

    def hidden_there(n, product):
        base = xrt[:, :, columns(n)].reshape(ROWS, 384).astype(F32)
        hid_p[:, columns(n)] = (base + product).astype(BF16)

    rback[...] = xrc[...].reshape(ROWS, WIDTH)
    tiles(rback, 0, 3, hidden_there)
    normed[...] = layer_norm(hid_p[...].astype(F32))
    tiles(ctx, 0, 3, hidden_here)

    stage(1, 4)
    stage(2, 3)
    stage(1, 5)

    def keep(n, product):
        qkv[lax.div(n, 3), :, columns(lax.rem(n, 3))] = product.astype(BF16)

    tiles(normed, 9, 7, keep)
    stage(2, 4)
    stage(2, 5)
    tiles(normed, 30, 2, lambda n, product: keep(n + 7, product))

    for i, tile in enumerate(attention(qkv.at[0], qkv.at[1], qkv.at[2], same)):
        for r in range(8):
            tctx[r, :, i * LANES : (i + 1) * LANES] = tile[16 * r : 16 * r + 16].astype(BF16)

    x_exchange(2, tctx, plane)
    x_wait(2, plane)
    moved = swap_rows(plane[...].reshape(ROWS, WIDTH), 8)
    for i in range(16):
        zback[0, i] = moved[8 * i : 8 * i + 8].astype(BF16)
    z_exchange(2, zback.at[0], zback.at[1])
    z_wait(2, zback.at[1])
    rback[...] = rows_of(zback.at[1])

    def last(n, product):
        out[:, columns(n)] = (hid_f[:, columns(n)].astype(F32) + product).astype(BF16)

    tiles(rback, 36, 3, last)

    for copy in sends:
        copy.wait_send()

    @pl.when(active)
    def _():
        for j in range(STEPS):
            for d in range(1, 8):
                spot = wts.at[j, x, y, zp]
                remote(spot, spot, p_s.at[j, d], p_r.at[j, zp], at(z, xc, y)).wait_send()

    @pl.when(jnp.logical_not(active))
    def _():
        remote(piece.at[x], gat.at[source], g_s.at[0], g_r.at[source], at(z, xc, y)).wait_send()


def shards(
    tokens,
    spatial_query,
    spatial_key,
    spatial_value,
    frame_counts,
    w_spatial_out,
    w_temporal_qkv,
    w_temporal_out,
):
    def padded(array, lanes):
        return jnp.pad(array, ((0, 16 - array.shape[0]), (0, lanes - array.shape[1])))

    wraw = jnp.concatenate(
        [padded(w_spatial_out, 384), padded(w_temporal_qkv, 896), padded(w_temporal_out, 512)], axis=1
    )
    flat = (ROWS, WIDTH)
    vmem = pl.BlockSpec(memory_space=pltpu.VMEM)
    dma = pltpu.SemaphoreType.DMA
    result = pl.pallas_call(
        kernel,
        out_shape=jax.ShapeDtypeStruct(flat, BF16),
        in_specs=[pl.BlockSpec(memory_space=pltpu.SMEM)] + [vmem] * 5,
        out_specs=vmem,
        scratch_shapes=[
            pltpu.VMEM((4, 16, RAW), BF16),
            pltpu.VMEM((4, STEPS, 16, LANES), BF16),
            pltpu.VMEM((16, STEPS, 16, LANES), BF16),
            pltpu.VMEM((STEPS, 4, 4, 8, PAIR, LANES), BF16),
            pltpu.VMEM((16, 8, WIDTH), BF16),
            pltpu.VMEM(flat, BF16),
            pltpu.VMEM((16, 8, WIDTH), BF16),
            pltpu.VMEM((16, 8, WIDTH), BF16),
            pltpu.VMEM((16, 8, WIDTH), BF16),
            pltpu.VMEM((8, 16, WIDTH), BF16),
            pltpu.VMEM((8, 16, WIDTH), BF16),
            pltpu.VMEM((8, 16, WIDTH), BF16),
            pltpu.VMEM((8, 16, WIDTH), BF16),
            pltpu.VMEM(flat, BF16),
            pltpu.VMEM(flat, BF16),
            pltpu.VMEM(flat, BF16),
            pltpu.VMEM((3,) + flat, BF16),
            pltpu.VMEM((8, 16, WIDTH), BF16),
            pltpu.VMEM(flat, BF16),
            pltpu.VMEM((8, 16, WIDTH), BF16),
            pltpu.VMEM((2, 16, 8, WIDTH), BF16),
            dma((4,)), dma((4,)),
            dma((8,)), dma((16,)),
            dma((STEPS, 8)), dma((STEPS, 8)),
            dma((STEPS, 2, 18)), dma((STEPS, 2, 18)),
            dma((3, 16)), dma((3, 16)),
            dma((3, 8)), dma((3, 8)),
        ],
        compiler_params=pltpu.CompilerParams(
            collective_id=0, has_side_effects=True, vmem_limit_bytes=50 * 2**20
        ),
    )(
        frame_counts,
        tokens.reshape(flat),
        spatial_query.reshape(flat),
        spatial_key.reshape(flat),
        spatial_value.reshape(flat),
        wraw,
    )
    return result.reshape(tokens.shape)


def solution(mesh):
    placed = (
        P("batch", "seq", None, None),
        P("batch", "seq", None, None),
        P("batch", "seq", None, None),
        P("batch", "seq", None, None),
        P("batch", None),
        P("seq", "batch"),
        P("seq", "batch"),
        P("seq", "batch"),
    )
    return jax.shard_map(
        shards, mesh=mesh, in_specs=placed, out_specs=P("batch", "seq", None, None), check_vma=False
    )
```

```python
import jax
import jax.numpy as jnp
from jax import lax
from jax.experimental import pallas as pl
from jax.experimental.pallas import tpu as pltpu
from jax.sharding import PartitionSpec as P

HEADS = 16
EPS = 1e-06
LOG2E = 1.4426950408889634
MESH = pl.DeviceIdType.MESH
BF16 = jnp.bfloat16
F32 = jnp.float32

ROWS = 128
WIDTH = 1152
SIZE = WIDTH // HEADS
LANES = 128
RAW = 1792
STEPS = 3
PAIR = 144
EARLY = 640

ORDER = list(range(9)) + [9, 10, 11, 18, 19, 20, 27]
ORDER += [28, 29, 12, 13, 14, 21, 22, 23, 30, 31, 32, 15, 16, 17, 24, 25]
ORDER += [26, 33, 34, 35] + list(range(36, 45)) + [44, 44, 44]


def dot(left, right):
    return jnp.dot(left, right, preferred_element_type=F32)


def iota(shape, dim):
    return lax.broadcasted_iota(jnp.int32, shape, dim)


def layer_norm(wide):
    mean = jnp.mean(wide, axis=1, keepdims=True)
    var = jnp.mean((wide - mean) ** 2, axis=1, keepdims=True)
    return ((wide - mean) * lax.rsqrt(var + EPS)).astype(BF16)


class Attention:
    def __init__(self, q_ref, k_ref, v_ref, same):
        self.q, self.k, self.v, self.same = q_ref, k_ref, v_ref, same
        self.parts = [[] for _ in range(WIDTH // LANES)]

    def heads(self, first, last):
        for head in range(first, last):
            low = SIZE * head
            start = low // LANES * LANES
            span = LANES if low + SIZE <= start + LANES else 2 * LANES
            window = slice(start, start + span)
            lane = iota((1, span), 1) + start
            own = jnp.where((lane >= low) & (lane < low + SIZE), 1.0, 0.0).astype(BF16)
            scores = lax.dot_general(
                self.q[:, window] * own, self.k[:, window], (((1,), (1,)), ((), ())), preferred_element_type=F32
            )
            if self.same is not None:
                scores = jnp.where(self.same, scores, -1e30)
            top = jnp.max(scores, axis=1, keepdims=True)
            raised = jnp.exp2((scores - top) * (SIZE**-0.5 * LOG2E))
            inverse = 1.0 / jnp.sum(raised, axis=1, keepdims=True)
            context = dot(raised.astype(BF16), self.v[:, window])
            for tile in range(span // LANES):
                value = context[:, tile * LANES : (tile + 1) * LANES] * inverse
                self.parts[start // LANES + tile].append((low + SIZE, value))

    def tile(self, index):
        lane = iota((ROWS, LANES), 1) + index * LANES
        found = self.parts[index]
        total = found[-1][1]
        for end, value in reversed(found[:-1]):
            total = jnp.where(lane < end, value, total)
        return total


def kernel(
    counts, tok_in, sq_in, sk_in, sv_in, wraw, out,
    tok, sq, sk, sv, raw, picks, piece, gat, wts, ctx, xt, xc_in, zst, zsc, zt, zc,
    hid_f, hid_p, normed, qkv, zs_a, zs_b, zr_a, zr_b, xs_a, xs_b, xr_a, xr_b, rback, total,
    in_s, y_s, y_r, g_s, g_r, p_s, p_r, w_s, w_r, z_s, z_r, x_s, x_r,
):
    me = lax.axis_index("seq")
    y = lax.axis_index("batch")
    z = lax.div(me, 8)
    xc = lax.rem(me, 8)
    x = lax.div(xc, 2)
    c = lax.rem(me, 2)
    zp = lax.div(z, 2)
    zpar = lax.rem(z, 2)
    zmate = z + 1 - 2 * zpar
    cstar = lax.div(z, 8)
    active = c == cstar

    def at(z2, xc2, y2):
        return {"seq": z2 * 8 + xc2, "batch": y2}

    def ring(value, step, size):
        return lax.rem(value + (step + size), size)

    def remote(src, dst, send, recv, device):
        return pltpu.make_async_remote_copy(
            src_ref=src, dst_ref=dst, send_sem=send, recv_sem=recv, device_id=device, device_id_type=MESH
        )

    sends = []
    maybe = []

    def send(src, dst, ss, rs, device):
        copy = remote(src, dst, ss, rs, device)
        copy.start()
        sends.append(copy)

    def send_if(on, src, dst, ss, rs, device):
        copy = remote(src, dst, ss, rs, device)
        pl.when(on)(copy.start)
        maybe.append((on, copy))

    def arrived(dst, ss, rs):
        remote(dst, dst, ss, rs, at(z, xc, y)).wait_recv()

    barrier = pltpu.get_barrier_semaphore()
    peers = [at(z, xc, ring(y, d, 4)) for d in (1, 2, 3)]
    peers += [at(z, ring(xc, d, 8), y) for d in range(1, 8)]
    peers += [at(zmate, ring(xc, d, 8), y) for d in range(1, 8)]
    peers += [at(ring(z, d, 16), xc, y) for d in range(1, 16)]
    for peer in peers:
        pl.semaphore_signal(barrier, inc=1, device_id=peer, device_id_type=MESH)

    loads = [
        pltpu.make_async_copy(src, dst, in_s.at[n])
        for n, (src, dst) in enumerate(
            ((wraw, raw.at[y]), (tok_in, tok), (sq_in, sq), (sk_in, sk), (sv_in, sv))
        )
    ]
    for load in loads:
        load.start()
    places = []
    row, col = iota((3 * LANES, LANES), 0), iota((3 * LANES, LANES), 1)
    for j in range(STEPS):
        for x2 in range(4):
            tile = sum(jnp.where(y == i, ORDER[16 * j + 4 * x2 + i], 0) for i in range(4))
            second = jnp.where(tile >= 9, 1, 0)
            third = jnp.where(tile >= 36, 1, 0)
            block = 288 + 576 * (second - third)
            lanes = 384 * second + 896 * third
            begin = LANES * (tile - 9 * second - 27 * third)
            y1 = jnp.where(second - third == 1, lax.div(begin, 864), lax.div(begin, 288))
            y2 = jnp.minimum(y1 + 1, 3)
            inside = begin - y1 * block
            skip = lax.rem(inside, LANES)
            first = jnp.minimum(block - inside, LANES)
            near = (row == col + skip) & (col < first)
            far = (row == col - first + 2 * LANES) & (col >= first)
            picks[j, x2] = jnp.where(near | far, 1.0, 0.0).astype(BF16)
            places.append((j, x2, y1, pl.multiple_of(lanes + inside - skip, LANES), y2, pl.multiple_of(lanes, LANES)))

    for load in loads[2:]:
        load.wait()
    spatial = Attention(sq, sk, sv, None)
    spatial.heads(0, HEADS)
    for i in range(9):
        ctx[:, i * LANES : (i + 1) * LANES] = spatial.tile(i).astype(BF16)
    loads[0].wait()
    loads[1].wait()

    pl.semaphore_wait(barrier, len(peers))

    for d in (1, 2, 3):
        send(raw.at[y], raw.at[y], y_s.at[d], y_r.at[y], at(z, xc, ring(y, d, 4)))

    def z_exchange(n, src, dst):
        for d in range(1, 16):
            to = ring(z, d, 16)
            send(src.at[to], dst.at[z], z_s.at[n, d], z_r.at[n, z], at(to, xc, y))
        dst[z] = src[z]

    def z_wait(n, dst):
        for d in range(1, 16):
            source = ring(z, d, 16)
            arrived(dst.at[source], z_s.at[n, d], z_r.at[n, source])

    def block(src, index):
        if len(src.shape) == 3:
            return src.at[index]
        return src.at[pl.ds(pl.multiple_of(index * 16, 16), 16)]

    def x_exchange(n, src, dst):
        for d in range(1, 8):
            to = ring(xc, d, 8)
            send(block(src, to), dst.at[xc], x_s.at[n, d], x_r.at[n, xc], at(z, to, y))
        dst[xc] = block(src, xc)[...]

    def x_wait(n, dst):
        for d in range(1, 8):
            source = ring(xc, d, 8)
            arrived(dst.at[source], x_s.at[n, d], x_r.at[n, source])

    def rows_of(ref):
        return jnp.concatenate([ref[i].astype(F32) for i in range(16)], axis=0).astype(BF16)

    def swap_rows(left, inner):
        outer = ROWS // inner
        i, k = iota((ROWS, ROWS), 0), iota((ROWS, ROWS), 1)
        pick = k == lax.rem(i, inner) * outer + lax.div(i, inner)
        return dot(jnp.where(pick, 1.0, 0.0).astype(BF16), left)

    x_exchange(0, ctx, xc_in)
    x_exchange(1, tok, xt)

    for d in (1, 2, 3):
        source = ring(y, d, 4)
        arrived(raw.at[source], y_s.at[d], y_r.at[source])

    for j, x2, y1, start1, y2, start2 in places:
        left = raw[y1, :, pl.ds(start1, 2 * LANES)]
        right = raw[y2, :, pl.ds(start2, LANES)]
        piece[x2, j] = dot(jnp.concatenate([left, right], axis=1), picks[j, x2]).astype(BF16)

    source = 8 * zpar + xc
    for zo in (0, 1):
        for dx in range(4):
            x2 = ring(x, dx, 4)
            where = at(z if zo == 0 else zmate, 2 * x2 + cstar, y)
            sem = g_s.at[4 * zo + dx]
            if zo == 0 and dx == 0:

                @pl.when(active)
                def _():
                    gat[source] = piece[x]

                send_if(jnp.logical_not(active), piece.at[x2], gat.at[source], sem, g_r.at[source], where)
            else:
                send(piece.at[x2], gat.at[source], sem, g_r.at[source], where)

    @pl.when(active)
    def _():
        for d in range(1, 16):
            other = ring(source, d, 16)
            arrived(gat.at[other], g_s.at[0], g_r.at[other])
        i, k = iota((PAIR, 256), 0), iota((PAIR, 256), 1)
        pick = jnp.where(k == 16 * lax.div(i, 9) + lax.rem(i, 9), 1.0, 0.0).astype(BF16)
        for j in range(STEPS):
            wts[j, x, y, zp] = dot(pick, gat[:, j].reshape(256, LANES)).astype(BF16)

    way = 2 * zpar - 1

    def passed(m):
        return ring(zp, -m * way, 8)

    def along(j, m, hops):
        block = passed(m)
        on = c == lax.div(block, 4)
        spot = wts.at[j, x, y, block]
        if m > 0:

            @pl.when(on)
            def _():
                arrived(spot, p_s.at[j, 0, 0], p_r.at[j, block])

        for hop in hops:
            to = ring(z, hop * way, 16)
            send_if(on, spot, spot, p_s.at[j, min(m, 1), hop - 1], p_r.at[j, block], at(to, xc, y))

    def to_z(n, landed, src, dst):
        x_wait(n, landed)
        moved = swap_rows(landed[...].reshape(ROWS, WIDTH), 8)
        for i in range(16):
            src[i] = moved[8 * i : 8 * i + 8].astype(BF16)
        z_exchange(n, src, dst)

    for j in range(STEPS):
        along(j, 0, (4, 3, 2, 1))
    to_z(0, xc_in, zsc, zc)
    along(0, 2, (3, 2, 1))
    to_z(1, xt, zst, zt)
    along(1, 2, (3, 2, 1))
    along(2, 2, (3, 2, 1))

    up, down = (lambda v: ring(v, 1, 4)), (lambda v: ring(v, -1, 4))
    far = lambda v: ring(v, 2, 4)

    def chain(j, order):
        base = 4 * c + 2 * order
        both, low, high = pl.ds(base, 2), pl.ds(base, 1), pl.ds(base + 1, 1)
        u, v = (x, y) if order == 0 else (y, x)

        def ref(uu, vv, part):
            if order == 0:
                return wts.at[j, uu, vv, part]
            return wts.at[j, vv, uu, part]

        def line(vv, part):
            if order == 0:
                return wts.at[j, :, vv, part]
            return wts.at[j, vv, :, part]

        def device(uu, vv):
            return at(z, 2 * uu + c, vv) if order == 0 else at(z, 2 * vv + c, uu)

        def go(n, spot, uu, vv):
            send(spot, spot, w_s.at[j, order, n], w_r.at[j, order, n], device(uu, vv))

        def got(n, spot):
            arrived(spot, w_s.at[j, order, n], w_r.at[j, order, n])

        def share(n, spot):
            send(spot, spot, w_s.at[j, order, n], w_r.at[j, order, n], at(z, 2 * x + 1 - c, y))

        def shared(n, vv):
            spot = (
                wts.at[j, :, vv, pl.ds(4 * (1 - c) + 2 * order, 2)]
                if order == 0
                else wts.at[j, vv, :, pl.ds(4 * (1 - c) + 2 * order, 2)]
            )
            arrived(spot, w_s.at[j, order, n], w_r.at[j, order, n])

        def s0():
            go(2, ref(u, v, both), far(u), v)
            go(0, ref(u, v, both), up(u), v)
            go(1, ref(u, v, both), down(u), v)
            go(4, ref(u, v, both), u, up(v))
            go(5, ref(u, v, both), u, down(v))

        def s1():
            got(0, ref(down(u), v, both))
            go(6, ref(down(u), v, both), u, up(v))
            go(7, ref(down(u), v, both), u, down(v))
            got(1, ref(up(u), v, both))
            go(8, ref(up(u), v, both), u, up(v))
            go(9, ref(up(u), v, both), u, down(v))
            got(2, ref(far(u), v, both))
            go(10, ref(far(u), v, both), u, up(v))
            go(11, ref(far(u), v, both), u, down(v))
            share(14, line(v, both))

        def s2():
            for k, uu in enumerate((u, down(u), up(u), far(u))):
                got(4 + 2 * k, ref(uu, down(v), both))
            go(12, line(down(v), low), u, up(v))
            share(15, line(down(v), both))
            for k, uu in enumerate((u, down(u), up(u), far(u))):
                got(5 + 2 * k, ref(uu, up(v), both))
            go(13, line(up(v), high), u, down(v))
            share(16, line(up(v), both))

        def s3():
            got(12, line(far(v), low))
            got(13, line(far(v), high))
            share(17, line(far(v), both))

        def s4():
            shared(14, v)
            shared(15, down(v))
            shared(16, up(v))
            shared(17, far(v))

        return s0, s1, s2, s3, s4

    chains = [[chain(j, 0), chain(j, 1)] for j in range(STEPS)]

    def stage(j, s):
        if s == 0:
            for m in (1, 3, 4, 5, 6, 7):
                block = passed(m)

                @pl.when(c == lax.div(block, 4))
                def _():
                    arrived(wts.at[j, x, y, block], p_s.at[j, 0, 0], p_r.at[j, block])

        chains[j][0][s]()
        chains[j][1][s]()

    def weights(first, count=3, depth=slice(0, WIDTH)):
        right = []
        for t in range(first, first + count):
            j, k = divmod(ORDER.index(t), 16)
            right.append(wts[j, k // 4, k % 4].reshape(WIDTH, LANES)[depth])
        return jnp.concatenate(right, axis=1)

    def columns(n):
        return slice(384 * n, 384 * n + 384)

    stage(0, 0)
    stage(1, 0)
    stage(0, 1)
    stage(2, 0)
    stage(1, 1)
    stage(0, 2)
    stage(2, 1)
    stage(0, 3)
    stage(1, 2)
    stage(0, 4)

    def clip_of(dim):
        frame = iota((ROWS, ROWS), dim)
        end = jnp.int32(0)
        clip = jnp.zeros((ROWS, ROWS), jnp.int32)
        for n in range(16):
            end = end + counts[0, n]
            clip = clip + jnp.where(frame >= end, 1, 0)
        return clip

    same = clip_of(0) == clip_of(1)

    z_wait(0, zc)
    rback[...] = rows_of(zc)
    z_wait(1, zt)
    total[...] = jnp.concatenate([zt[i].astype(F32) for i in range(16)], axis=0)
    for n in range(3):
        hid_p[:, columns(n)] = (total[:, columns(n)] + dot(rback[...], weights(3 * n))).astype(BF16)
    stage(1, 3)
    stage(2, 2)
    normed[...] = layer_norm(hid_p[...].astype(F32))
    for n in range(3):
        hid_f[:, columns(n)] = (tok[:, columns(n)].astype(F32) + dot(ctx[...], weights(3 * n))).astype(BF16)

    stage(1, 4)

    def project(part, first, count=3):
        product = dot(normed[...], weights(9 + 9 * part + first, count))
        qkv[part, :, LANES * first : LANES * (first + count)] = product.astype(BF16)

    def return_z(n, tiles, src, dst):
        for i, t in enumerate(tiles):
            tile = temporal.tile(t)
            for r in range(16):
                src[r, :, i * LANES : (i + 1) * LANES] = tile[8 * r : 8 * r + 8].astype(BF16)
        z_exchange(n, src, dst)

    def return_x(n, landed, src, dst):
        z_wait(n, landed)
        moved = swap_rows(rows_of(landed), 16)
        for i in range(8):
            src[i] = moved[16 * i : 16 * i + 16].astype(BF16)
        x_exchange(n, src, dst)

    for part, first in ((0, 0), (1, 0), (2, 0), (0, 3), (1, 3), (2, 3), (0, 6)):
        project(part, first)
    project(1, 6, 2)
    temporal = Attention(qkv.at[0], qkv.at[1], qkv.at[2], same)
    temporal.heads(0, 10)
    return_z(2, range(5), zs_a, zr_a)
    stage(2, 3)
    stage(2, 4)
    project(1, 8, 1)
    project(2, 6)
    temporal.heads(10, 16)
    return_z(3, range(5, 9), zs_b, zr_b)
    return_x(2, zr_a, xs_a, xr_a)
    return_x(3, zr_b, xs_b, xr_b)

    x_wait(2, xr_a)
    rback[:, :EARLY] = xr_a[...].reshape(ROWS, EARLY)
    for n in range(3):
        product = dot(rback[:, :EARLY], weights(36 + 3 * n, 3, slice(0, EARLY)))
        total[:, columns(n)] = hid_f[:, columns(n)].astype(F32) + product
    x_wait(3, xr_b)
    rback[:, EARLY:] = xr_b[...].reshape(ROWS, WIDTH - EARLY)
    for n in range(3):
        product = dot(rback[:, EARLY:], weights(36 + 3 * n, 3, slice(EARLY, WIDTH)))
        out[:, columns(n)] = (total[:, columns(n)] + product).astype(BF16)

    for copy in sends:
        copy.wait_send()
    for on, copy in maybe:
        pl.when(on)(copy.wait_send)


def shards(
    tokens,
    spatial_query,
    spatial_key,
    spatial_value,
    frame_counts,
    w_spatial_out,
    w_temporal_qkv,
    w_temporal_out,
):
    def padded(array, lanes):
        return jnp.pad(array, ((0, 16 - array.shape[0]), (0, lanes - array.shape[1])))

    wraw = jnp.concatenate(
        [padded(w_spatial_out, 384), padded(w_temporal_qkv, 896), padded(w_temporal_out, 512)], axis=1
    )
    flat = (ROWS, WIDTH)
    vmem = pl.BlockSpec(memory_space=pltpu.VMEM)
    late = WIDTH - EARLY
    dma = pltpu.SemaphoreType.DMA
    result = pl.pallas_call(
        kernel,
        out_shape=jax.ShapeDtypeStruct(flat, BF16),
        in_specs=[pl.BlockSpec(memory_space=pltpu.SMEM)] + [pl.BlockSpec(memory_space=pl.ANY)] * 5,
        out_specs=vmem,
        scratch_shapes=[
            *[pltpu.VMEM(flat, BF16)] * 4,
            pltpu.VMEM((4, 16, RAW), BF16),
            pltpu.VMEM((STEPS, 4, 3 * LANES, LANES), BF16),
            pltpu.VMEM((4, STEPS, 16, LANES), BF16),
            pltpu.VMEM((16, STEPS, 16, LANES), BF16),
            pltpu.VMEM((STEPS, 4, 4, 8, PAIR, LANES), BF16),
            pltpu.VMEM(flat, BF16),
            pltpu.VMEM((8, 16, WIDTH), BF16),
            pltpu.VMEM((8, 16, WIDTH), BF16),
            *[pltpu.VMEM((16, 8, WIDTH), BF16)] * 4,
            pltpu.VMEM(flat, BF16),
            pltpu.VMEM(flat, BF16),
            pltpu.VMEM(flat, BF16),
            pltpu.VMEM((3,) + flat, BF16),
            pltpu.VMEM((16, 8, EARLY), BF16),
            pltpu.VMEM((16, 8, late), BF16),
            pltpu.VMEM((16, 8, EARLY), BF16),
            pltpu.VMEM((16, 8, late), BF16),
            pltpu.VMEM((8, 16, EARLY), BF16),
            pltpu.VMEM((8, 16, late), BF16),
            pltpu.VMEM((8, 16, EARLY), BF16),
            pltpu.VMEM((8, 16, late), BF16),
            pltpu.VMEM(flat, BF16),
            pltpu.VMEM(flat, F32),
            dma((5,)),
            dma((4,)), dma((4,)),
            dma((8,)), dma((16,)),
            dma((STEPS, 2, 4)), dma((STEPS, 8)),
            dma((STEPS, 2, 18)), dma((STEPS, 2, 18)),
            dma((4, 16)), dma((4, 16)),
            dma((4, 8)), dma((4, 8)),
        ],
        compiler_params=pltpu.CompilerParams(
            collective_id=0, has_side_effects=True, vmem_limit_bytes=50 * 2**20
        ),
    )(
        frame_counts,
        tokens.reshape(flat),
        spatial_query.reshape(flat),
        spatial_key.reshape(flat),
        spatial_value.reshape(flat),
        wraw,
    )
    return result.reshape(tokens.shape)


def solution(mesh):
    placed = (
        P("batch", "seq", None, None),
        P("batch", "seq", None, None),
        P("batch", "seq", None, None),
        P("batch", "seq", None, None),
        P("batch", None),
        P("seq", "batch"),
        P("seq", "batch"),
        P("seq", "batch"),
    )
    return jax.shard_map(
        shards, mesh=mesh, in_specs=placed, out_specs=P("batch", "seq", None, None), check_vma=False
    )
```

```python
import jax
import jax.numpy as jnp
from jax import lax
from jax.experimental import pallas as pl
from jax.experimental.pallas import tpu as pltpu
from jax.sharding import PartitionSpec as P

HEADS = 16
EPS = 1e-06
LOG2E = 1.4426950408889634
MESH = pl.DeviceIdType.MESH
BF16 = jnp.bfloat16
F32 = jnp.float32

ROWS = 128
WIDTH = 1152
SIZE = WIDTH // HEADS
LANES = 128
RAW = 1792
STEPS = 3
PAIR = 144
CHUNK = 384

ORDER = list(range(9)) + [9, 10, 11, 18, 19, 20, 27]
ORDER += [28, 29, 12, 13, 14, 15, 21, 22, 23, 24, 30, 31, 32, 33, 16, 25]
ORDER += [17, 26, 34, 35] + list(range(36, 45)) + [44, 44, 44]


def dot(left, right):
    return jnp.dot(left, right, preferred_element_type=F32)


def iota(shape, dim):
    return lax.broadcasted_iota(jnp.int32, shape, dim)


def layer_norm(wide):
    mean = jnp.mean(wide, axis=1, keepdims=True)
    var = jnp.mean((wide - mean) ** 2, axis=1, keepdims=True)
    return ((wide - mean) * lax.rsqrt(var + EPS)).astype(BF16)


class Attention:
    def __init__(self, q_ref, k_ref, v_ref, same):
        self.q, self.k, self.v, self.same = q_ref, k_ref, v_ref, same
        self.parts = [[] for _ in range(WIDTH // LANES)]

    def heads(self, first, last):
        for head in range(first, last):
            low = SIZE * head
            start = low // LANES * LANES
            span = LANES if low + SIZE <= start + LANES else 2 * LANES
            window = slice(start, start + span)
            lane = iota((1, span), 1) + start
            own = jnp.where((lane >= low) & (lane < low + SIZE), 1.0, 0.0).astype(BF16)
            scores = lax.dot_general(
                self.q[:, window] * own, self.k[:, window], (((1,), (1,)), ((), ())), preferred_element_type=F32
            )
            if self.same is not None:
                scores = jnp.where(self.same, scores, -1e30)
            top = jnp.max(scores, axis=1, keepdims=True)
            raised = jnp.exp2((scores - top) * (SIZE**-0.5 * LOG2E))
            inverse = 1.0 / jnp.sum(raised, axis=1, keepdims=True)
            context = dot(raised.astype(BF16), self.v[:, window])
            for tile in range(span // LANES):
                value = context[:, tile * LANES : (tile + 1) * LANES] * inverse
                self.parts[start // LANES + tile].append((low + SIZE, value))

    def tile(self, index):
        lane = iota((ROWS, LANES), 1) + index * LANES
        found = self.parts[index]
        total = found[-1][1]
        for end, value in reversed(found[:-1]):
            total = jnp.where(lane < end, value, total)
        return total


def kernel(
    counts, tok_in, sq_in, sk_in, sv_in, wraw, out,
    tok, sq, sk, sv, raw, picks, piece, gat, wts, ctx, xt, xc_in, zst, zsc, zt, zc,
    hid_f, hid_p, normed, qkv, zs, zr, xs, xr, rback, total,
    in_s, y_s, y_r, g_s, g_r, p_s, p_r, w_s, w_r, z_s, z_r, x_s, x_r,
):
    me = lax.axis_index("seq")
    y = lax.axis_index("batch")
    z = lax.div(me, 8)
    xc = lax.rem(me, 8)
    x = lax.div(xc, 2)
    c = lax.rem(me, 2)
    zp = lax.div(z, 2)
    zpar = lax.rem(z, 2)
    zmate = z + 1 - 2 * zpar
    cstar = lax.div(z, 8)
    active = c == cstar

    def at(z2, xc2, y2):
        return {"seq": z2 * 8 + xc2, "batch": y2}

    def ring(value, step, size):
        return lax.rem(value + (step + size), size)

    def remote(src, dst, send, recv, device):
        return pltpu.make_async_remote_copy(
            src_ref=src, dst_ref=dst, send_sem=send, recv_sem=recv, device_id=device, device_id_type=MESH
        )

    sends = []
    maybe = []

    def send(src, dst, ss, rs, device):
        copy = remote(src, dst, ss, rs, device)
        copy.start()
        sends.append(copy)

    def send_if(on, src, dst, ss, rs, device):
        copy = remote(src, dst, ss, rs, device)
        pl.when(on)(copy.start)
        maybe.append((on, copy))

    def arrived(dst, ss, rs):
        remote(dst, dst, ss, rs, at(z, xc, y)).wait_recv()

    barrier = pltpu.get_barrier_semaphore()
    peers = [at(z, xc, ring(y, d, 4)) for d in (1, 2, 3)]
    peers += [at(z, ring(xc, d, 8), y) for d in range(1, 8)]
    peers += [at(zmate, ring(xc, d, 8), y) for d in range(1, 8)]
    peers += [at(ring(z, d, 16), xc, y) for d in range(1, 16)]
    for peer in peers:
        pl.semaphore_signal(barrier, inc=1, device_id=peer, device_id_type=MESH)

    loads = [
        pltpu.make_async_copy(src, dst, in_s.at[n])
        for n, (src, dst) in enumerate(
            ((wraw, raw.at[y]), (tok_in, tok), (sq_in, sq), (sk_in, sk), (sv_in, sv))
        )
    ]
    for load in loads:
        load.start()
    loads[0].wait()
    pl.semaphore_wait(barrier, len(peers))

    for d in (1, 2, 3):
        send(raw.at[y], raw.at[y], y_s.at[d], y_r.at[y], at(z, xc, ring(y, d, 4)))

    def z_exchange(n, src, dst):
        for d in range(1, 16):
            to = ring(z, d, 16)
            send(src.at[to], dst.at[z], z_s.at[n, d], z_r.at[n, z], at(to, xc, y))
        dst[z] = src[z]

    def z_wait(n, dst):
        for d in range(1, 16):
            source = ring(z, d, 16)
            arrived(dst.at[source], z_s.at[n, d], z_r.at[n, source])

    def block(src, index):
        if len(src.shape) == 3:
            return src.at[index]
        return src.at[pl.ds(pl.multiple_of(index * 16, 16), 16)]

    def x_exchange(n, src, dst):
        for d in range(1, 8):
            to = ring(xc, d, 8)
            send(block(src, to), dst.at[xc], x_s.at[n, d], x_r.at[n, xc], at(z, to, y))
        dst[xc] = block(src, xc)[...]

    def x_wait(n, dst):
        for d in range(1, 8):
            source = ring(xc, d, 8)
            arrived(dst.at[source], x_s.at[n, d], x_r.at[n, source])

    def rows_of(ref):
        return jnp.concatenate([ref[i].astype(F32) for i in range(16)], axis=0).astype(BF16)

    def swap_rows(left, inner):
        outer = ROWS // inner
        i, k = iota((ROWS, ROWS), 0), iota((ROWS, ROWS), 1)
        pick = k == lax.rem(i, inner) * outer + lax.div(i, inner)
        return dot(jnp.where(pick, 1.0, 0.0).astype(BF16), left)

    loads[1].wait()
    x_exchange(1, tok, xt)

    places = []
    row, col = iota((3 * LANES, LANES), 0), iota((3 * LANES, LANES), 1)
    for j in range(STEPS):
        for x2 in range(4):
            tile = sum(jnp.where(y == i, ORDER[16 * j + 4 * x2 + i], 0) for i in range(4))
            second = jnp.where(tile >= 9, 1, 0)
            third = jnp.where(tile >= 36, 1, 0)
            held = 288 + 576 * (second - third)
            lanes = 384 * second + 896 * third
            begin = LANES * (tile - 9 * second - 27 * third)
            y1 = jnp.where(second - third == 1, lax.div(begin, 864), lax.div(begin, 288))
            y2 = jnp.minimum(y1 + 1, 3)
            inside = begin - y1 * held
            skip = lax.rem(inside, LANES)
            first = jnp.minimum(held - inside, LANES)
            near = (row == col + skip) & (col < first)
            far = (row == col - first + 2 * LANES) & (col >= first)
            picks[j, x2] = jnp.where(near | far, 1.0, 0.0).astype(BF16)
            places.append((j, x2, y1, pl.multiple_of(lanes + inside - skip, LANES), y2, pl.multiple_of(lanes, LANES)))

    for d in (1, 2, 3):
        source = ring(y, d, 4)
        arrived(raw.at[source], y_s.at[d], y_r.at[source])

    for j, x2, y1, start1, y2, start2 in places:
        left = raw[y1, :, pl.ds(start1, 2 * LANES)]
        right = raw[y2, :, pl.ds(start2, LANES)]
        piece[x2, j] = dot(jnp.concatenate([left, right], axis=1), picks[j, x2]).astype(BF16)

    def to_z(n, landed, src, dst):
        x_wait(n, landed)
        moved = swap_rows(landed[...].reshape(ROWS, WIDTH), 8)
        for i in range(16):
            src[i] = moved[8 * i : 8 * i + 8].astype(BF16)
        z_exchange(n, src, dst)

    source = 8 * zpar + xc
    for zo in (0, 1):
        for dx in range(4):
            x2 = ring(x, dx, 4)
            where = at(z if zo == 0 else zmate, 2 * x2 + cstar, y)
            sem = g_s.at[4 * zo + dx]
            if zo == 0 and dx == 0:

                @pl.when(active)
                def _():
                    gat[source] = piece[x]

                send_if(jnp.logical_not(active), piece.at[x2], gat.at[source], sem, g_r.at[source], where)
            else:
                send(piece.at[x2], gat.at[source], sem, g_r.at[source], where)

    for load in loads[2:]:
        load.wait()
    spatial = Attention(sq, sk, sv, None)
    spatial.heads(0, 4)

    @pl.when(active)
    def _():
        for d in range(1, 16):
            other = ring(source, d, 16)
            arrived(gat.at[other], g_s.at[0], g_r.at[other])
        i, k = iota((PAIR, 256), 0), iota((PAIR, 256), 1)
        pick = jnp.where(k == 16 * lax.div(i, 9) + lax.rem(i, 9), 1.0, 0.0).astype(BF16)
        for j in range(STEPS):
            wts[j, x, y, zp] = dot(pick, gat[:, j].reshape(256, LANES)).astype(BF16)

    way = 2 * zpar - 1

    def passed(m):
        return ring(zp, -m * way, 8)

    def along(j, m, hops):
        block = passed(m)
        on = c == lax.div(block, 4)
        spot = wts.at[j, x, y, block]
        if m > 0:

            @pl.when(on)
            def _():
                arrived(spot, p_s.at[j, 0, 0], p_r.at[j, block])

        for hop in hops:
            to = ring(z, hop * way, 16)
            send_if(on, spot, spot, p_s.at[j, min(m, 1), hop - 1], p_r.at[j, block], at(to, xc, y))

    along(0, 0, (4, 3, 2, 1))
    spatial.heads(4, 8)
    along(0, 2, (3, 2, 1))
    to_z(1, xt, zst, zt)
    along(1, 0, (4, 3, 2, 1))
    along(2, 0, (4, 3, 2, 1))
    spatial.heads(8, HEADS)
    for i in range(9):
        ctx[:, i * LANES : (i + 1) * LANES] = spatial.tile(i).astype(BF16)
    x_exchange(0, ctx, xc_in)

    up, down = (lambda v: ring(v, 1, 4)), (lambda v: ring(v, -1, 4))
    far = lambda v: ring(v, 2, 4)

    def chain(j, order):
        base = 4 * c + 2 * order
        both, low, high = pl.ds(base, 2), pl.ds(base, 1), pl.ds(base + 1, 1)
        u, v = (x, y) if order == 0 else (y, x)

        def ref(uu, vv, part):
            if order == 0:
                return wts.at[j, uu, vv, part]
            return wts.at[j, vv, uu, part]

        def line(vv, part):
            if order == 0:
                return wts.at[j, :, vv, part]
            return wts.at[j, vv, :, part]

        def device(uu, vv):
            return at(z, 2 * uu + c, vv) if order == 0 else at(z, 2 * vv + c, uu)

        def go(n, spot, uu, vv):
            send(spot, spot, w_s.at[j, order, n], w_r.at[j, order, n], device(uu, vv))

        def got(n, spot):
            arrived(spot, w_s.at[j, order, n], w_r.at[j, order, n])

        def share(n, spot):
            send(spot, spot, w_s.at[j, order, n], w_r.at[j, order, n], at(z, 2 * x + 1 - c, y))

        def shared(n, vv):
            spot = (
                wts.at[j, :, vv, pl.ds(4 * (1 - c) + 2 * order, 2)]
                if order == 0
                else wts.at[j, vv, :, pl.ds(4 * (1 - c) + 2 * order, 2)]
            )
            arrived(spot, w_s.at[j, order, n], w_r.at[j, order, n])

        def s0():
            go(2, ref(u, v, both), far(u), v)
            go(0, ref(u, v, both), up(u), v)
            go(1, ref(u, v, both), down(u), v)
            go(4, ref(u, v, both), u, up(v))
            go(5, ref(u, v, both), u, down(v))

        def s1():
            got(0, ref(down(u), v, both))
            go(6, ref(down(u), v, both), u, up(v))
            go(7, ref(down(u), v, both), u, down(v))
            got(1, ref(up(u), v, both))
            go(8, ref(up(u), v, both), u, up(v))
            go(9, ref(up(u), v, both), u, down(v))
            got(2, ref(far(u), v, both))
            go(10, ref(far(u), v, both), u, up(v))
            go(11, ref(far(u), v, both), u, down(v))
            share(14, line(v, both))

        def s2():
            for k, uu in enumerate((u, down(u), up(u), far(u))):
                got(4 + 2 * k, ref(uu, down(v), both))
            go(12, line(down(v), low), u, up(v))
            share(15, line(down(v), both))
            for k, uu in enumerate((u, down(u), up(u), far(u))):
                got(5 + 2 * k, ref(uu, up(v), both))
            go(13, line(up(v), high), u, down(v))
            share(16, line(up(v), both))

        def s3():
            got(12, line(far(v), low))
            got(13, line(far(v), high))
            share(17, line(far(v), both))

        def s4():
            shared(14, v)
            shared(15, down(v))
            shared(16, up(v))
            shared(17, far(v))

        return s0, s1, s2, s3, s4

    chains = [[chain(j, 0), chain(j, 1)] for j in range(STEPS)]

    def stage(j, s):
        if s == 0:
            for m in (1, 3, 4, 5, 6, 7):
                block = passed(m)

                @pl.when(c == lax.div(block, 4))
                def _():
                    arrived(wts.at[j, x, y, block], p_s.at[j, 0, 0], p_r.at[j, block])

        chains[j][0][s]()
        chains[j][1][s]()

    def weights(first, count=3, depth=slice(0, WIDTH)):
        right = []
        for t in range(first, first + count):
            j, k = divmod(ORDER.index(t), 16)
            right.append(wts[j, k // 4, k % 4].reshape(WIDTH, LANES)[depth])
        return jnp.concatenate(right, axis=1)

    def columns(n):
        return slice(384 * n, 384 * n + 384)

    stage(0, 0)
    along(1, 2, (3, 2, 1))
    along(2, 2, (3, 2, 1))
    to_z(0, xc_in, zsc, zc)
    stage(0, 1)
    stage(1, 0)
    stage(0, 2)
    stage(1, 1)
    stage(0, 3)
    stage(2, 0)
    stage(1, 2)
    stage(0, 4)

    def clip_of(dim):
        frame = iota((ROWS, ROWS), dim)
        end = jnp.int32(0)
        clip = jnp.zeros((ROWS, ROWS), jnp.int32)
        for n in range(16):
            end = end + counts[0, n]
            clip = clip + jnp.where(frame >= end, 1, 0)
        return clip

    same = clip_of(0) == clip_of(1)

    z_wait(0, zc)
    rback[...] = rows_of(zc)
    z_wait(1, zt)
    total[...] = jnp.concatenate([zt[i].astype(F32) for i in range(16)], axis=0)
    for n in range(3):
        hid_p[:, columns(n)] = (total[:, columns(n)] + dot(rback[...], weights(3 * n))).astype(BF16)
    stage(1, 3)
    stage(2, 1)
    normed[...] = layer_norm(hid_p[...].astype(F32))
    stage(1, 4)
    def project(part, first, count=3):
        product = dot(normed[...], weights(9 + 9 * part + first, count))
        qkv[part, :, LANES * first : LANES * (first + count)] = product.astype(BF16)

    def return_z(n):
        for i in range(3):
            tile = temporal.tile(3 * n + i)
            for r in range(16):
                zs[n, r, :, i * LANES : (i + 1) * LANES] = tile[8 * r : 8 * r + 8].astype(BF16)
        z_exchange(2 + n, zs.at[n], zr.at[n])

    def return_x(n):
        z_wait(2 + n, zr.at[n])
        moved = swap_rows(rows_of(zr.at[n]), 16)
        for i in range(8):
            xs[n, i] = moved[16 * i : 16 * i + 16].astype(BF16)
        x_exchange(2 + n, xs.at[n], xr.at[n])

    for part in range(3):
        project(part, 0)
        project(part, 3)
        project(part, 6, 1 if part == 2 else 2)
    temporal = Attention(qkv.at[0], qkv.at[1], qkv.at[2], same)
    temporal.heads(0, 6)
    return_z(0)
    stage(2, 2)
    temporal.heads(6, 11)
    return_z(1)
    for n in range(3):
        hid_f[:, columns(n)] = (tok[:, columns(n)].astype(F32) + dot(ctx[...], weights(3 * n))).astype(BF16)
    stage(2, 3)
    stage(2, 4)
    project(0, 8, 1)
    project(1, 8, 1)
    project(2, 7, 2)
    temporal.heads(11, HEADS)
    return_z(2)
    return_x(0)
    return_x(1)
    return_x(2)

    for part in range(3):
        x_wait(2 + part, xr.at[part])
        rback[:, :CHUNK] = xr[part].reshape(ROWS, CHUNK)
        depth = slice(part * CHUNK, part * CHUNK + CHUNK)
        for n in range(3):
            before = hid_f[:, columns(n)].astype(F32) if part == 0 else total[:, columns(n)]
            after = before + dot(rback[:, :CHUNK], weights(36 + 3 * n, 3, depth))
            if part < 2:
                total[:, columns(n)] = after
            else:
                out[:, columns(n)] = after.astype(BF16)

    for copy in sends:
        copy.wait_send()
    for on, copy in maybe:
        pl.when(on)(copy.wait_send)


def shards(
    tokens,
    spatial_query,
    spatial_key,
    spatial_value,
    frame_counts,
    w_spatial_out,
    w_temporal_qkv,
    w_temporal_out,
):
    def padded(array, lanes):
        return jnp.pad(array, ((0, 16 - array.shape[0]), (0, lanes - array.shape[1])))

    wraw = jnp.concatenate(
        [padded(w_spatial_out, 384), padded(w_temporal_qkv, 896), padded(w_temporal_out, 512)], axis=1
    )
    flat = (ROWS, WIDTH)
    vmem = pl.BlockSpec(memory_space=pltpu.VMEM)
    dma = pltpu.SemaphoreType.DMA
    result = pl.pallas_call(
        kernel,
        out_shape=jax.ShapeDtypeStruct(flat, BF16),
        in_specs=[pl.BlockSpec(memory_space=pltpu.SMEM)] + [pl.BlockSpec(memory_space=pl.ANY)] * 5,
        out_specs=vmem,
        scratch_shapes=[
            *[pltpu.VMEM(flat, BF16)] * 4,
            pltpu.VMEM((4, 16, RAW), BF16),
            pltpu.VMEM((STEPS, 4, 3 * LANES, LANES), BF16),
            pltpu.VMEM((4, STEPS, 16, LANES), BF16),
            pltpu.VMEM((16, STEPS, 16, LANES), BF16),
            pltpu.VMEM((STEPS, 4, 4, 8, PAIR, LANES), BF16),
            pltpu.VMEM(flat, BF16),
            pltpu.VMEM((8, 16, WIDTH), BF16),
            pltpu.VMEM((8, 16, WIDTH), BF16),
            *[pltpu.VMEM((16, 8, WIDTH), BF16)] * 4,
            pltpu.VMEM(flat, BF16),
            pltpu.VMEM(flat, BF16),
            pltpu.VMEM(flat, BF16),
            pltpu.VMEM((3,) + flat, BF16),
            *[pltpu.VMEM((3, 16, 8, CHUNK), BF16)] * 2,
            *[pltpu.VMEM((3, 8, 16, CHUNK), BF16)] * 2,
            pltpu.VMEM(flat, BF16),
            pltpu.VMEM(flat, F32),
            dma((5,)),
            dma((4,)), dma((4,)),
            dma((8,)), dma((16,)),
            dma((STEPS, 2, 7)), dma((STEPS, 8)),
            dma((STEPS, 2, 18)), dma((STEPS, 2, 18)),
            dma((5, 16)), dma((5, 16)),
            dma((5, 8)), dma((5, 8)),
        ],
        compiler_params=pltpu.CompilerParams(
            collective_id=0, has_side_effects=True, vmem_limit_bytes=50 * 2**20
        ),
    )(
        frame_counts,
        tokens.reshape(flat),
        spatial_query.reshape(flat),
        spatial_key.reshape(flat),
        spatial_value.reshape(flat),
        wraw,
    )
    return result.reshape(tokens.shape)


def solution(mesh):
    placed = (
        P("batch", "seq", None, None),
        P("batch", "seq", None, None),
        P("batch", "seq", None, None),
        P("batch", "seq", None, None),
        P("batch", None),
        P("seq", "batch"),
        P("seq", "batch"),
        P("seq", "batch"),
    )
    return jax.shard_map(
        shards, mesh=mesh, in_specs=placed, out_specs=P("batch", "seq", None, None), check_vma=False
    )
```

```python
import jax
import jax.numpy as jnp
from jax import lax
from jax.experimental import pallas as pl
from jax.experimental.pallas import tpu as pltpu
from jax.sharding import PartitionSpec as P

HEADS = 16
EPS = 1e-06
LOG2E = 1.4426950408889634
MESH = pl.DeviceIdType.MESH
BF16 = jnp.bfloat16
F32 = jnp.float32

ROWS = 128
WIDTH = 1152
SIZE = WIDTH // HEADS
LANES = 128
RAW = 1792
STEPS = 3
PAIR = 144
CHUNK = 384

ORDER = list(range(9)) + [9, 10, 11, 18, 19, 20, 27]
ORDER += [28, 29, 12, 13, 14, 15, 21, 22, 23, 24, 30, 31, 32, 33, 16, 25]
ORDER += [17, 26, 34, 35] + list(range(36, 45)) + [44, 44, 44]


def dot(left, right):
    return jnp.dot(left, right, preferred_element_type=F32)


def iota(shape, dim):
    return lax.broadcasted_iota(jnp.int32, shape, dim)


def layer_norm(wide):
    mean = jnp.mean(wide, axis=1, keepdims=True)
    var = jnp.mean((wide - mean) ** 2, axis=1, keepdims=True)
    return ((wide - mean) * lax.rsqrt(var + EPS)).astype(BF16)


class Attention:
    def __init__(self, q_ref, k_ref, v_ref, same):
        self.q, self.k, self.v, self.same = q_ref, k_ref, v_ref, same
        self.parts = [[] for _ in range(WIDTH // LANES)]

    def heads(self, first, last):
        for head in range(first, last):
            low = SIZE * head
            start = low // LANES * LANES
            span = LANES if low + SIZE <= start + LANES else 2 * LANES
            window = slice(start, start + span)
            lane = iota((1, span), 1) + start
            own = jnp.where((lane >= low) & (lane < low + SIZE), 1.0, 0.0).astype(BF16)
            scores = lax.dot_general(
                self.q[:, window] * own, self.k[:, window], (((1,), (1,)), ((), ())), preferred_element_type=F32
            )
            if self.same is not None:
                scores = jnp.where(self.same, scores, -1e30)
            top = jnp.max(scores, axis=1, keepdims=True)
            raised = jnp.exp2((scores - top) * (SIZE**-0.5 * LOG2E))
            inverse = 1.0 / jnp.sum(raised, axis=1, keepdims=True)
            context = dot(raised.astype(BF16), self.v[:, window])
            for tile in range(span // LANES):
                value = context[:, tile * LANES : (tile + 1) * LANES] * inverse
                self.parts[start // LANES + tile].append((low + SIZE, value))

    def tile(self, index):
        lane = iota((ROWS, LANES), 1) + index * LANES
        found = self.parts[index]
        total = found[-1][1]
        for end, value in reversed(found[:-1]):
            total = jnp.where(lane < end, value, total)
        return total


def kernel(
    counts, tok_in, sq_in, sk_in, sv_in, wraw, out,
    tok, sq, sk, sv, raw, picks, piece, gat, wts, ctx, xt, xc_in, zst, zsc, zt, zc,
    hid_f, hid_p, normed, qkv, zs, zr, xs, xr, rback, total,
    in_s, y_s, y_r, g_s, g_r, p_s, p_r, w_s, w_r, z_s, z_r, x_s, x_r,
):
    me = lax.axis_index("seq")
    y = lax.axis_index("batch")
    z = lax.div(me, 8)
    xc = lax.rem(me, 8)
    x = lax.div(xc, 2)
    c = lax.rem(me, 2)
    zp = lax.div(z, 2)
    zpar = lax.rem(z, 2)
    zmate = z + 1 - 2 * zpar
    cstar = lax.div(z, 8)
    active = c == cstar

    def at(z2, xc2, y2):
        return {"seq": z2 * 8 + xc2, "batch": y2}

    def ring(value, step, size):
        return lax.rem(value + (step + size), size)

    def remote(src, dst, send, recv, device):
        return pltpu.make_async_remote_copy(
            src_ref=src, dst_ref=dst, send_sem=send, recv_sem=recv, device_id=device, device_id_type=MESH
        )

    sends = []
    maybe = []

    def send(src, dst, ss, rs, device):
        copy = remote(src, dst, ss, rs, device)
        copy.start()
        sends.append(copy)

    def send_if(on, src, dst, ss, rs, device):
        copy = remote(src, dst, ss, rs, device)
        pl.when(on)(copy.start)
        maybe.append((on, copy))

    def arrived(dst, ss, rs):
        remote(dst, dst, ss, rs, at(z, xc, y)).wait_recv()

    barrier = pltpu.get_barrier_semaphore()
    peers = [at(z, xc, ring(y, d, 4)) for d in (1, 2, 3)]
    peers += [at(z, ring(xc, d, 8), y) for d in range(1, 8)]
    peers += [at(zmate, ring(xc, d, 8), y) for d in range(1, 8)]
    peers += [at(ring(z, d, 16), xc, y) for d in range(1, 16)]
    for peer in peers:
        pl.semaphore_signal(barrier, inc=1, device_id=peer, device_id_type=MESH)

    loads = [
        pltpu.make_async_copy(src, dst, in_s.at[n])
        for n, (src, dst) in enumerate(
            ((wraw, raw.at[y]), (tok_in, tok), (sq_in, sq), (sk_in, sk), (sv_in, sv))
        )
    ]
    for load in loads:
        load.start()
    loads[0].wait()
    pl.semaphore_wait(barrier, len(peers))

    for d in (1, 2, 3):
        send(raw.at[y], raw.at[y], y_s.at[d], y_r.at[y], at(z, xc, ring(y, d, 4)))

    def z_exchange(n, src, dst):
        for d in range(1, 16):
            to = ring(z, d, 16)
            send(src.at[to], dst.at[z], z_s.at[n, d], z_r.at[n, z], at(to, xc, y))
        dst[z] = src[z]

    def z_wait(n, dst):
        for d in range(1, 16):
            source = ring(z, d, 16)
            arrived(dst.at[source], z_s.at[n, d], z_r.at[n, source])

    def block(src, index):
        if len(src.shape) == 3:
            return src.at[index]
        return src.at[pl.ds(pl.multiple_of(index * 16, 16), 16)]

    def x_exchange(n, src, dst):
        for d in range(1, 8):
            to = ring(xc, d, 8)
            send(block(src, to), dst.at[xc], x_s.at[n, d], x_r.at[n, xc], at(z, to, y))
        dst[xc] = block(src, xc)[...]

    def x_wait(n, dst):
        for d in range(1, 8):
            source = ring(xc, d, 8)
            arrived(dst.at[source], x_s.at[n, d], x_r.at[n, source])

    def rows_of(ref):
        return jnp.concatenate([ref[i].astype(F32) for i in range(16)], axis=0).astype(BF16)

    def swap_rows(left, inner):
        outer = ROWS // inner
        i, k = iota((ROWS, ROWS), 0), iota((ROWS, ROWS), 1)
        pick = k == lax.rem(i, inner) * outer + lax.div(i, inner)
        return dot(jnp.where(pick, 1.0, 0.0).astype(BF16), left)

    loads[1].wait()
    x_exchange(1, tok, xt)

    places = []
    row, col = iota((3 * LANES, LANES), 0), iota((3 * LANES, LANES), 1)
    for j in range(STEPS):
        for x2 in range(4):
            tile = sum(jnp.where(y == i, ORDER[16 * j + 4 * x2 + i], 0) for i in range(4))
            second = jnp.where(tile >= 9, 1, 0)
            third = jnp.where(tile >= 36, 1, 0)
            held = 288 + 576 * (second - third)
            lanes = 384 * second + 896 * third
            begin = LANES * (tile - 9 * second - 27 * third)
            y1 = jnp.where(second - third == 1, lax.div(begin, 864), lax.div(begin, 288))
            y2 = jnp.minimum(y1 + 1, 3)
            inside = begin - y1 * held
            skip = lax.rem(inside, LANES)
            first = jnp.minimum(held - inside, LANES)
            near = (row == col + skip) & (col < first)
            far = (row == col - first + 2 * LANES) & (col >= first)
            picks[j, x2] = jnp.where(near | far, 1.0, 0.0).astype(BF16)
            places.append((j, x2, y1, pl.multiple_of(lanes + inside - skip, LANES), y2, pl.multiple_of(lanes, LANES)))

    for d in (1, 2, 3):
        source = ring(y, d, 4)
        arrived(raw.at[source], y_s.at[d], y_r.at[source])

    for j, x2, y1, start1, y2, start2 in places:
        left = raw[y1, :, pl.ds(start1, 2 * LANES)]
        right = raw[y2, :, pl.ds(start2, LANES)]
        piece[x2, j] = dot(jnp.concatenate([left, right], axis=1), picks[j, x2]).astype(BF16)

    def to_z(n, landed, src, dst):
        x_wait(n, landed)
        moved = swap_rows(landed[...].reshape(ROWS, WIDTH), 8)
        for i in range(16):
            src[i] = moved[8 * i : 8 * i + 8].astype(BF16)
        z_exchange(n, src, dst)

    source = 8 * zpar + xc
    for zo in (0, 1):
        for dx in range(4):
            x2 = ring(x, dx, 4)
            where = at(z if zo == 0 else zmate, 2 * x2 + cstar, y)
            sem = g_s.at[4 * zo + dx]
            if zo == 0 and dx == 0:

                @pl.when(active)
                def _():
                    gat[source] = piece[x]

                send_if(jnp.logical_not(active), piece.at[x2], gat.at[source], sem, g_r.at[source], where)
            else:
                send(piece.at[x2], gat.at[source], sem, g_r.at[source], where)

    for load in loads[2:]:
        load.wait()
    spatial = Attention(sq, sk, sv, None)
    spatial.heads(0, 4)

    @pl.when(active)
    def _():
        for d in range(1, 16):
            other = ring(source, d, 16)
            arrived(gat.at[other], g_s.at[0], g_r.at[other])
        i, k = iota((PAIR, 256), 0), iota((PAIR, 256), 1)
        pick = jnp.where(k == 16 * lax.div(i, 9) + lax.rem(i, 9), 1.0, 0.0).astype(BF16)
        for j in range(STEPS):
            wts[j, x, y, zp] = dot(pick, gat[:, j].reshape(256, LANES)).astype(BF16)

    way = 2 * zpar - 1

    def passed(m):
        return ring(zp, -m * way, 8)

    def along(j, m, hops):
        block = passed(m)
        on = c == lax.div(block, 4)
        spot = wts.at[j, x, y, block]
        if m > 0:

            @pl.when(on)
            def _():
                arrived(spot, p_s.at[j, 0, 0], p_r.at[j, block])

        for hop in hops:
            to = ring(z, hop * way, 16)
            send_if(on, spot, spot, p_s.at[j, min(m, 1), hop - 1], p_r.at[j, block], at(to, xc, y))

    along(0, 0, (4, 3, 2, 1))
    spatial.heads(4, 8)
    along(0, 2, (3, 2, 1))
    to_z(1, xt, zst, zt)
    along(1, 0, (4, 3, 2, 1))
    along(2, 0, (4, 3, 2, 1))
    spatial.heads(8, HEADS)
    for i in range(9):
        ctx[:, i * LANES : (i + 1) * LANES] = spatial.tile(i).astype(BF16)
    x_exchange(0, ctx, xc_in)

    up, down = (lambda v: ring(v, 1, 4)), (lambda v: ring(v, -1, 4))
    far = lambda v: ring(v, 2, 4)

    def chain(j, order):
        base = 4 * c + 2 * order
        both, low, high = pl.ds(base, 2), pl.ds(base, 1), pl.ds(base + 1, 1)
        u, v = (x, y) if order == 0 else (y, x)

        def ref(uu, vv, part):
            if order == 0:
                return wts.at[j, uu, vv, part]
            return wts.at[j, vv, uu, part]

        def line(vv, part):
            if order == 0:
                return wts.at[j, :, vv, part]
            return wts.at[j, vv, :, part]

        def device(uu, vv):
            return at(z, 2 * uu + c, vv) if order == 0 else at(z, 2 * vv + c, uu)

        def go(n, spot, uu, vv):
            send(spot, spot, w_s.at[j, order, n], w_r.at[j, order, n], device(uu, vv))

        def got(n, spot):
            arrived(spot, w_s.at[j, order, n], w_r.at[j, order, n])

        def share(n, spot):
            send(spot, spot, w_s.at[j, order, n], w_r.at[j, order, n], at(z, 2 * x + 1 - c, y))

        def shared(n, vv):
            spot = (
                wts.at[j, :, vv, pl.ds(4 * (1 - c) + 2 * order, 2)]
                if order == 0
                else wts.at[j, vv, :, pl.ds(4 * (1 - c) + 2 * order, 2)]
            )
            arrived(spot, w_s.at[j, order, n], w_r.at[j, order, n])

        def s0():
            go(2, ref(u, v, both), far(u), v)
            go(0, ref(u, v, both), up(u), v)
            go(1, ref(u, v, both), down(u), v)
            go(4, ref(u, v, both), u, up(v))
            go(5, ref(u, v, both), u, down(v))

        def s1():
            got(0, ref(down(u), v, both))
            go(6, ref(down(u), v, both), u, up(v))
            go(7, ref(down(u), v, both), u, down(v))
            got(1, ref(up(u), v, both))
            go(8, ref(up(u), v, both), u, up(v))
            go(9, ref(up(u), v, both), u, down(v))
            got(2, ref(far(u), v, both))
            go(10, ref(far(u), v, both), u, up(v))
            go(11, ref(far(u), v, both), u, down(v))
            share(14, line(v, both))

        def s2():
            for k, uu in enumerate((u, down(u), up(u), far(u))):
                got(4 + 2 * k, ref(uu, down(v), both))
            go(12, line(down(v), low), u, up(v))
            share(15, line(down(v), both))
            for k, uu in enumerate((u, down(u), up(u), far(u))):
                got(5 + 2 * k, ref(uu, up(v), both))
            go(13, line(up(v), high), u, down(v))
            share(16, line(up(v), both))

        def s3():
            got(12, line(far(v), low))
            got(13, line(far(v), high))
            share(17, line(far(v), both))

        def s4():
            shared(14, v)
            shared(15, down(v))
            shared(16, up(v))
            shared(17, far(v))

        return s0, s1, s2, s3, s4

    chains = [[chain(j, 0), chain(j, 1)] for j in range(STEPS)]

    def stage(j, s):
        if s == 0:
            for m in (1, 3, 4, 5, 6, 7):
                block = passed(m)

                @pl.when(c == lax.div(block, 4))
                def _():
                    arrived(wts.at[j, x, y, block], p_s.at[j, 0, 0], p_r.at[j, block])

        chains[j][0][s]()
        chains[j][1][s]()

    def weights(first, count=3, depth=slice(0, WIDTH)):
        right = []
        for t in range(first, first + count):
            j, k = divmod(ORDER.index(t), 16)
            right.append(wts[j, k // 4, k % 4].reshape(WIDTH, LANES)[depth])
        return jnp.concatenate(right, axis=1)

    def columns(n):
        return slice(384 * n, 384 * n + 384)

    stage(0, 0)
    along(1, 2, (3, 2, 1))
    along(2, 2, (3, 2, 1))
    to_z(0, xc_in, zsc, zc)
    stage(0, 1)
    stage(1, 0)
    stage(0, 2)
    stage(1, 1)
    stage(0, 3)
    stage(2, 0)
    stage(1, 2)
    stage(0, 4)

    def clip_of(dim):
        frame = iota((ROWS, ROWS), dim)
        end = jnp.int32(0)
        clip = jnp.zeros((ROWS, ROWS), jnp.int32)
        for n in range(16):
            end = end + counts[0, n]
            clip = clip + jnp.where(frame >= end, 1, 0)
        return clip

    same = clip_of(0) == clip_of(1)

    z_wait(0, zc)
    rback[...] = rows_of(zc)
    z_wait(1, zt)
    total[...] = jnp.concatenate([zt[i].astype(F32) for i in range(16)], axis=0)
    for n in range(3):
        hid_p[:, columns(n)] = (total[:, columns(n)] + dot(rback[...], weights(3 * n))).astype(BF16)
    stage(1, 3)
    stage(2, 1)
    normed[...] = layer_norm(hid_p[...].astype(F32))
    stage(1, 4)
    def project(part, first, count=3):
        product = dot(normed[...], weights(9 + 9 * part + first, count))
        qkv[part, :, LANES * first : LANES * (first + count)] = product.astype(BF16)

    def return_z(n):
        for i in range(3):
            tile = temporal.tile(3 * n + i)
            for r in range(16):
                zs[n, r, :, i * LANES : (i + 1) * LANES] = tile[8 * r : 8 * r + 8].astype(BF16)
        z_exchange(2 + n, zs.at[n], zr.at[n])

    def return_x(n):
        z_wait(2 + n, zr.at[n])
        moved = swap_rows(rows_of(zr.at[n]), 16)
        for i in range(8):
            xs[n, i] = moved[16 * i : 16 * i + 16].astype(BF16)
        x_exchange(2 + n, xs.at[n], xr.at[n])

    for part in range(3):
        project(part, 0)
        project(part, 3)
        project(part, 6, 1 if part == 2 else 2)
    temporal = Attention(qkv.at[0], qkv.at[1], qkv.at[2], same)
    temporal.heads(0, 6)
    return_z(0)
    stage(2, 2)
    temporal.heads(6, 11)
    return_z(1)
    for n in range(3):
        hid_f[:, columns(n)] = (tok[:, columns(n)].astype(F32) + dot(ctx[...], weights(3 * n))).astype(BF16)
    stage(2, 3)
    stage(2, 4)
    project(0, 8, 1)
    project(1, 8, 1)
    project(2, 7, 2)
    temporal.heads(11, HEADS)
    return_z(2)
    settled = len(sends)
    return_x(0)
    return_x(1)
    return_x(2)
    for copy in sends[:settled]:
        copy.wait_send()
    for on, copy in maybe:
        pl.when(on)(copy.wait_send)

    for part in range(3):
        x_wait(2 + part, xr.at[part])
        rback[:, :CHUNK] = xr[part].reshape(ROWS, CHUNK)
        depth = slice(part * CHUNK, part * CHUNK + CHUNK)
        for n in range(3):
            before = hid_f[:, columns(n)].astype(F32) if part == 0 else total[:, columns(n)]
            after = before + dot(rback[:, :CHUNK], weights(36 + 3 * n, 3, depth))
            if part < 2:
                total[:, columns(n)] = after
            else:
                out[:, columns(n)] = after.astype(BF16)

    for copy in sends[settled:]:
        copy.wait_send()


def shards(
    tokens,
    spatial_query,
    spatial_key,
    spatial_value,
    frame_counts,
    w_spatial_out,
    w_temporal_qkv,
    w_temporal_out,
):
    def padded(array, lanes):
        return jnp.pad(array, ((0, 16 - array.shape[0]), (0, lanes - array.shape[1])))

    wraw = jnp.concatenate(
        [padded(w_spatial_out, 384), padded(w_temporal_qkv, 896), padded(w_temporal_out, 512)], axis=1
    )
    flat = (ROWS, WIDTH)
    vmem = pl.BlockSpec(memory_space=pltpu.VMEM)
    dma = pltpu.SemaphoreType.DMA
    result = pl.pallas_call(
        kernel,
        out_shape=jax.ShapeDtypeStruct(flat, BF16),
        in_specs=[pl.BlockSpec(memory_space=pltpu.SMEM)] + [pl.BlockSpec(memory_space=pl.ANY)] * 5,
        out_specs=vmem,
        scratch_shapes=[
            *[pltpu.VMEM(flat, BF16)] * 4,
            pltpu.VMEM((4, 16, RAW), BF16),
            pltpu.VMEM((STEPS, 4, 3 * LANES, LANES), BF16),
            pltpu.VMEM((4, STEPS, 16, LANES), BF16),
            pltpu.VMEM((16, STEPS, 16, LANES), BF16),
            pltpu.VMEM((STEPS, 4, 4, 8, PAIR, LANES), BF16),
            pltpu.VMEM(flat, BF16),
            pltpu.VMEM((8, 16, WIDTH), BF16),
            pltpu.VMEM((8, 16, WIDTH), BF16),
            *[pltpu.VMEM((16, 8, WIDTH), BF16)] * 4,
            pltpu.VMEM(flat, BF16),
            pltpu.VMEM(flat, BF16),
            pltpu.VMEM(flat, BF16),
            pltpu.VMEM((3,) + flat, BF16),
            *[pltpu.VMEM((3, 16, 8, CHUNK), BF16)] * 2,
            *[pltpu.VMEM((3, 8, 16, CHUNK), BF16)] * 2,
            pltpu.VMEM(flat, BF16),
            pltpu.VMEM(flat, F32),
            dma((5,)),
            dma((4,)), dma((4,)),
            dma((8,)), dma((16,)),
            dma((STEPS, 2, 7)), dma((STEPS, 8)),
            dma((STEPS, 2, 18)), dma((STEPS, 2, 18)),
            dma((5, 16)), dma((5, 16)),
            dma((5, 8)), dma((5, 8)),
        ],
        compiler_params=pltpu.CompilerParams(
            collective_id=0, has_side_effects=True, vmem_limit_bytes=50 * 2**20
        ),
    )(
        frame_counts,
        tokens.reshape(flat),
        spatial_query.reshape(flat),
        spatial_key.reshape(flat),
        spatial_value.reshape(flat),
        wraw,
    )
    return result.reshape(tokens.shape)


def solution(mesh):
    placed = (
        P("batch", "seq", None, None),
        P("batch", "seq", None, None),
        P("batch", "seq", None, None),
        P("batch", "seq", None, None),
        P("batch", None),
        P("seq", "batch"),
        P("seq", "batch"),
        P("seq", "batch"),
    )
    return jax.shard_map(
        shards, mesh=mesh, in_specs=placed, out_specs=P("batch", "seq", None, None), check_vma=False
    )
```
